128 devices in a mesh: dp: 16 (over x_hi, y, core), tensor: 8 (over x_lo, z).
Axes of the slice: x: 4 (x_hi: 2, x_lo: 2; x = x_hi * 2 + x_lo), y: 4, z: 4, core: 2. Of those that a mesh axis runs over, the one named last changes fastest.
Arguments:
- gate_pre: bfloat16 [32, 512, 14336], P('dp', None, 'tensor'), may hold values from -6 to 6
- up_val: bfloat16 [32, 512, 14336], P('dp', None, 'tensor'), may hold values from -6 to 6
- layer_in: bfloat16 [32, 512, 4096], P('dp', None, 'tensor'), may hold values from -6 to 6
- out_grad: bfloat16 [32, 512, 4096], P('dp'), may hold values from -0.29882812 to 0.29882812
- down_weight: bfloat16 [14336, 4096], P('tensor', 'dp'), may hold values from -0.09375 to 0.09375
- down_in_proj: bfloat16 [14336, 64], P('tensor'), may hold values from -0.046875 to 0.046875
- down_out_proj: bfloat16 [4096, 64], replicated, may hold values from -0.09375 to 0.09375
- up_in_proj: bfloat16 [4096, 64], P('tensor'), may hold values from -0.09375 to 0.09375
- up_out_proj: bfloat16 [14336, 64], P('tensor'), may hold values from -0.046875 to 0.046875
- counts: int32 [32], P('dp'), may hold values from 128 to 512, as said below
- assignment: int32 [32], P('dp'), may hold values from 0 to 31, each once
- queries: int32 [8], replicated, may hold values from 0 to 31
Outputs:
- projected: float32 [2, 32, 4096], P(None, 'dp')
- gram: float32 [2, 32, 32], replicated
- scores: float32 [2, 8, 32], replicated
The draws below stay inside these ranges and needn't reach their ends.
Inputs may be any that keep to these rules, and one draw needn't show every extreme that they name: `counts`: some example has 512 live tokens and some has 128.
All inputs are finite; a program needn't handle non-finite values.
Results may differ from the reference program's by a relative error of at most 0.003.
Values may be sent and summed in bfloat16 or wider, within the bound.
No kernel may reach another device: no remote copies, remote signals or barrier semaphores. Data moves between devices by JAX's collectives and lax.ppermute only.
A program may use at most 128 MiB of HBM per device.

```python
import jax
import jax.numpy as jnp
from jax import lax

D = 4096
FF = 14336
RANK = 64
SEQ = 512
QUERIES = 8
EXAMPLES = 32
KDIM = 4096


def draw_counts(key, part):
    key = jax.random.fold_in(key, 7)
    first, second = jax.random.split(key)
    base = jax.random.randint(first, (EXAMPLES,), SEQ // 4, SEQ + 1)
    spots = jax.random.permutation(second, EXAMPLES)
    base = base.at[spots[0]].set(SEQ).at[spots[1]].set(SEQ // 4)
    return base.astype(jnp.int32)


def with_ends(drawn, stream_key, smallest, high):
    longest = drawn.shape.index(max(drawn.shape))
    spots = []
    for shift in (0, 1):
        where = [jax.random.randint(jax.random.fold_in(stream_key, axis), (), 0, length) for axis, length in enumerate(drawn.shape)]
        where[longest] = (where[longest] + shift) % drawn.shape[longest]
        spots.append(tuple(where))
    return drawn.at[spots[0]].set(smallest).at[spots[1]].set(high)


def block_scale(rng, extent, cuts, smallest, high):
    gain = 1.0
    for dim, parts in cuts:
        steps = jax.random.uniform(jax.random.fold_in(jax.random.fold_in(rng, 6), dim), (parts,), jnp.float32, smallest / len(cuts), high / len(cuts))
        gain = gain * jnp.repeat(jnp.exp(steps), extent[dim] // parts).reshape((-1,) + (1,) * (len(extent) - 1 - dim))
    return gain


def centred(rng, extent, scale, reach, pieces=(), held_as=jnp.bfloat16):
    entries = scale * jax.random.normal(rng, extent, jnp.float32)
    if pieces:
        entries = entries * block_scale(rng, extent, pieces, -0.22, 0.18)
    return jnp.clip(entries, -reach, reach).astype(held_as)


def setup_inputs(seed: int = 0) -> dict:
    key_of = jax.random.split(jax.random.key(seed), 13)
    gate_pre = centred(key_of[0], (EXAMPLES, SEQ, FF), 1.0, 6.0, ((0, 16), (2, 8)))
    up_val = centred(key_of[1], (EXAMPLES, SEQ, FF), 1.0, 6.0, ((0, 16), (2, 8)))
    layer_in = centred(key_of[2], (EXAMPLES, SEQ, D), 1.0, 6.0, ((0, 16), (2, 8)))
    out_grad = centred(key_of[3], (EXAMPLES, SEQ, D), 0.05, 0.29882812, ((0, 16),))
    down_weight = centred(key_of[4], (FF, D), D ** -0.5, 0.09375, ((0, 8), (1, 16)))
    down_in_proj = centred(key_of[5], (FF, RANK), FF ** -0.5, 0.046875, ((0, 8),))
    down_out_proj = centred(key_of[6], (D, RANK), D ** -0.5, 0.09375)
    up_in_proj = centred(key_of[7], (D, RANK), D ** -0.5, 0.09375, ((0, 8),))
    up_out_proj = centred(key_of[8], (FF, RANK), FF ** -0.5, 0.046875, ((0, 8),))
    counts = draw_counts(jax.random.fold_in(key_of[12], 71), 0)
    assignment = jax.random.permutation(key_of[10], EXAMPLES).astype(jnp.int32)
    queries = with_ends(jax.random.randint(key_of[11], (QUERIES,), 0, EXAMPLES), jax.random.fold_in(key_of[11], 1), 0, EXAMPLES - 1).astype(jnp.int32)
    return {"gate_pre": gate_pre, "up_val": up_val, "layer_in": layer_in, "out_grad": out_grad, "down_weight": down_weight, "down_in_proj": down_in_proj, "down_out_proj": down_out_proj, "up_in_proj": up_in_proj, "up_out_proj": up_out_proj, "counts": counts, "assignment": assignment, "queries": queries}


def one_example(args, down_weight, down_in_proj, down_out_proj, up_in_proj, up_out_proj):
    gate_row, up_row, in_row, grad_row, count = args
    act = jax.nn.silu(gate_row.astype(jnp.float32))
    hidden = (act * up_row.astype(jnp.float32)).astype(jnp.bfloat16)
    back = jnp.dot(grad_row, down_weight.T, preferred_element_type=jnp.float32)
    delta = (back * act).astype(jnp.bfloat16)
    hid_rows = jnp.dot(hidden, down_in_proj, preferred_element_type=jnp.float32)
    out_rows = jnp.dot(grad_row, down_out_proj, preferred_element_type=jnp.float32)
    in_rows = jnp.dot(in_row, up_in_proj, preferred_element_type=jnp.float32)
    del_rows = jnp.dot(delta, up_out_proj, preferred_element_type=jnp.float32)
    live = (jnp.arange(SEQ, dtype=jnp.int32) < count).astype(jnp.float32)
    first = jnp.einsum('ti,tj->ij', hid_rows * live[:, None], out_rows, precision=lax.Precision.HIGHEST)
    second = jnp.einsum('ti,tj->ij', in_rows * live[:, None], del_rows, precision=lax.Precision.HIGHEST)
    return jnp.stack([first.reshape(-1), second.reshape(-1)])

def reference(gate_pre, up_val, layer_in, out_grad, down_weight, down_in_proj, down_out_proj, up_in_proj, up_out_proj, counts, assignment, queries):

    def step(args):
        return one_example(args, down_weight, down_in_proj, down_out_proj, up_in_proj, up_out_proj)
    stacked = lax.map(step, (gate_pre, up_val, layer_in, out_grad, counts))
    projected = jnp.transpose(stacked, (1, 0, 2))
    byid = jnp.zeros_like(projected).at[:, assignment].set(projected)
    gram = jnp.einsum('mak,mbk->mab', byid, byid, precision=lax.Precision.HIGHEST) / float(KDIM)
    norm = jnp.sqrt(jnp.diagonal(gram, axis1=1, axis2=2) + 1e-06)
    scores = gram[:, queries, :] / (norm[:, queries][:, :, None] * norm[:, None, :])
    return (projected, gram, scores)
```

```python
import functools

import jax
import jax.numpy as jnp
from jax import lax
from jax.experimental import pallas as pl
from jax.experimental.pallas import tpu as pltpu
from jax.sharding import PartitionSpec as P

AXES = ("dp", "tensor")
BF16, F32 = jnp.bfloat16, jnp.float32
HIGHEST = lax.Precision.HIGHEST
TILE = 512
EARLY_TILE = 256
NT = (((1,), (1,)), ((), ()))
CHUNKS = ((0, 896),)
SMALL = pl.CostEstimate(flops=1000, bytes_accessed=1000, transcendentals=0)


def coords(i):
    dp, tensor = divmod(i, 8)
    x_hi, rest = divmod(dp, 8)
    y, core = divmod(rest, 2)
    x_lo, z = divmod(tensor, 4)
    return x_hi * 2 + x_lo, y, z, core


def index(x, y, z, core):
    x_hi, x_lo = divmod(x % 4, 2)
    return ((x_hi * 4 + y % 4) * 2 + core) * 8 + x_lo * 4 + z % 4


def pair(v, phase):
    return (v ^ 1) if phase == 0 else (v + (1 if v % 2 else -1)) % 4


def moved(value, to):
    return lax.ppermute(value, AXES, [(i, index(*to(*coords(i)))) for i in range(128)])


def swap_core(v):
    return moved(v, lambda x, y, z, c: (x, y, z, 1 - c))


def swap_y(v, step):
    return moved(v, lambda x, y, z, c: (x, pair(y, step ^ c), z, c))


def swap_z(v, step):
    return moved(v, lambda x, y, z, c: (x, y, pair(z, step ^ c), c))


def swap_x(v, phase):
    return moved(v, lambda x, y, z, c: (pair(x, phase), y, z, c))


def swap_x_far(v):
    return moved(v, lambda x, y, z, c: (x + 2, y, z, c))


def silu(v):
    half = 0.5 * v
    return half + half * jnp.tanh(half)


def after(value, *others):
    def nothing(*refs):
        pass

    anywhere = pl.BlockSpec(memory_space=pl.ANY)
    return pl.pallas_call(
        nothing,
        out_shape=jax.ShapeDtypeStruct(value.shape, value.dtype),
        in_specs=[anywhere] * (1 + len(others)),
        out_specs=anywhere,
        input_output_aliases={0: 0},
        name="after",
    )(value, *others)


def rows_kernel(counts, gate, up, grad, inp, din_t, dout_t, uin_t, _, out):
    i = pl.program_id(0)
    per = 512 // EARLY_TILE
    act = silu(gate[...].astype(F32))
    hidden = (act * up[...].astype(F32)).astype(BF16)
    hid_t = lax.dot_general(din_t[...], hidden, NT, preferred_element_type=F32)
    in_t = lax.dot_general(uin_t[...], inp[...], NT, preferred_element_type=F32)
    out_rows = lax.dot_general(grad[...], dout_t[...], NT, preferred_element_type=F32)
    pos = (i % per) * EARLY_TILE + lax.broadcasted_iota(jnp.int32, (64, EARLY_TILE), 1)
    live = (pos < counts[i // per]).astype(F32)
    first = jnp.dot(hid_t * live, out_rows, precision=HIGHEST, preferred_element_type=F32)
    packed = jnp.concatenate([first[:32], first[32:]], axis=1)
    here = pl.ds(pl.multiple_of((i // per) * 32, 32), 32)

    @pl.when(i % per == 0)
    def _():
        out[here, 1024:] = packed

    @pl.when(i % per != 0)
    def _():
        out[here, 1024:] += packed

    out[:, pl.ds(pl.multiple_of(i * EARLY_TILE, EARLY_TILE), EARLY_TILE)] = in_t * live


def projected_rows(counts, gate, up, grad, inp, din_t, dout_t, uin_t, later_than):
    tokens, width = gate.shape
    row = lambda n: pl.BlockSpec((EARLY_TILE, n), lambda i, s: (i, 0))
    full = lambda a: pl.BlockSpec(a.shape, lambda i, s: (0, 0))
    return pl.pallas_call(
        rows_kernel,
        out_shape=jax.ShapeDtypeStruct((64, tokens + 128), F32),
        grid_spec=pltpu.PrefetchScalarGridSpec(
            num_scalar_prefetch=1,
            grid=(tokens // EARLY_TILE,),
            in_specs=[row(width), row(width), row(grad.shape[1]), row(inp.shape[1]), full(din_t), full(dout_t), full(uin_t), pl.BlockSpec(memory_space=pl.ANY)],
            out_specs=pl.BlockSpec((64, tokens + 128), lambda i, s: (0, 0)),
        ),
        compiler_params=pltpu.CompilerParams(vmem_limit_bytes=56 * 2**20),
        cost_estimate=SMALL,
        name="early_rows",
    )(counts, gate, up, grad, inp, din_t, dout_t, uin_t, later_than)


def back_kernel(n, has_acc, last, has_first, lo, cols, *refs):
    i = pl.program_id(0)
    half = pl.num_programs(0) // 2
    refs = list(refs)
    acc_ref = refs.pop(0) if has_acc else None
    blocks, rest = refs[: 3 * n], refs[3 * n :]
    out = rest[-1]

    def run(side):
        acc = acc_ref[...] if has_acc else None
        for p in range(n):
            term = lax.dot_general(blocks[3 * p + side][...], blocks[3 * p + 2][...], NT, preferred_element_type=F32)
            acc = term if acc is None else acc + term
        if not last:
            out[...] = acc
            return
        width = acc.shape[1]
        gate = rest[side][:, lo : lo + width]
        delta = (acc * silu(gate.astype(F32))).astype(BF16)
        del_rows = lax.dot_general(delta, rest[2][:, lo : lo + width], NT, preferred_element_type=F32)
        second = jnp.dot(rest[3 + side][...], del_rows, precision=HIGHEST, preferred_element_type=F32)
        packed = jnp.concatenate([second[:32], second[32:]], axis=1)

        @pl.when(i % (512 // TILE) == 0)
        def _():
            out[0] = packed + rest[5][0] if has_first else packed

        @pl.when(i % (512 // TILE) != 0)
        def _():
            out[0] += packed

    @pl.when(i < half)
    def _():
        run(0)

    @pl.when(i >= half)
    def _():
        run(1)


def back_step(cols, acc, pieces, grads, tail=None, lo=0):
    mine, theirs = grads
    tokens = mine.shape[0]
    steps = tokens // TILE
    width = pieces[0][0].shape[0]
    feats = pieces[0][0].shape[1]
    own_row = lambda i: jnp.minimum(i, steps - 1)
    other_row = lambda i: jnp.maximum(i - steps, 0)
    args, specs = [], []
    acc_spec = pl.BlockSpec((TILE, width), lambda i, s: (i, 0))
    if acc is not None:
        args.append(acc)
        specs.append(acc_spec)
    for weight, k in pieces:
        args += [mine, theirs, weight]
        specs += [
            pl.BlockSpec((TILE, feats), lambda i, s, k=k: (own_row(i), s[k])),
            pl.BlockSpec((TILE, feats), lambda i, s, k=k: (other_row(i), s[k])),
            pl.BlockSpec((width, feats), lambda i, s: (0, 0)),
        ]
    n = len(pieces)
    if tail is None:
        out_shape = jax.ShapeDtypeStruct((2 * tokens, width), F32)
        out_spec = acc_spec
    else:
        gate_mine, gate_theirs, proj, rows_mine, rows_theirs, first = tail
        hid = gate_mine.shape[1] // 2
        args += [gate_mine, gate_theirs, proj, rows_mine, rows_theirs]
        specs += [
            pl.BlockSpec((TILE, hid), lambda i, s: (own_row(i), s[8])),
            pl.BlockSpec((TILE, hid), lambda i, s: (other_row(i), s[8])),
            pl.BlockSpec((64, hid), lambda i, s: (0, s[8])),
            pl.BlockSpec((64, TILE), lambda i, s: (0, own_row(i))),
            pl.BlockSpec((64, TILE), lambda i, s: (0, other_row(i))),
        ]
        out_spec = pl.BlockSpec((1, 32, 128), lambda i, s: ((i // (512 // TILE) + 2 * s[8]) % 4, 0, 0))
        if first is not None:
            args.append(first)
            specs.append(out_spec)
        out_shape = jax.ShapeDtypeStruct((4, 32, 128), F32)
    return pl.pallas_call(
        functools.partial(back_kernel, n, acc is not None, tail is not None, tail is not None and tail[5] is not None, lo),
        out_shape=out_shape,
        grid_spec=pltpu.PrefetchScalarGridSpec(
            num_scalar_prefetch=1, grid=(2 * steps,), in_specs=specs, out_specs=out_spec
        ),
        compiler_params=pltpu.CompilerParams(vmem_limit_bytes=56 * 2**20),
        cost_estimate=SMALL,
        name="back_last" if tail is not None else "back_part",
    )(cols, *args)


def body(
    gate_pre, up_val, layer_in, out_grad, down_weight, down_in_proj, down_out_proj,
    up_in_proj, up_out_proj, counts, assignment, queries,
):
    ex_dev, seq_len, width_ff = gate_pre.shape
    tokens = ex_dev * seq_len
    half = width_ff // 2
    dp = lax.axis_index("dp")
    core = dp % 2
    y = (dp // 2) % 4
    x_hi = dp // 8

    def partner(v, step):
        odd = (step ^ core) == 0
        return jnp.where(odd, v ^ 1, (v + jnp.where(v % 2 == 1, 1, 3)) % 4)

    y1, y2 = partner(y, 0), partner(y, 1)
    y12 = partner(y2, 0)
    here, there = x_hi * 4, (1 - x_hi) * 4
    cols = jnp.stack(
        [here + y, here + y1, here + y2, there + y, here + y12, there + y2, there + y1, there + y12, core]
    ).astype(jnp.int32)

    gate = gate_pre.reshape(tokens, width_ff)
    up = up_val.reshape(tokens, width_ff)
    grads = out_grad.reshape(tokens, -1)
    inputs = layer_in.reshape(tokens, -1)

    weight_other = swap_core(down_weight)
    ids_other = swap_core(assignment)
    is_even = core == 0
    even = jnp.concatenate([down_weight[:half], weight_other[:half]], axis=1)
    odd = jnp.concatenate([weight_other[half:], down_weight[half:]], axis=1)
    h = jnp.where(is_even, even, odd)

    h_x = swap_x_far(h)
    h_y = swap_y(h, 0)
    h_y2 = swap_y(h, 1)
    gate_other = swap_core(gate)
    grads_other = swap_core(grads)
    both = (grads, grads_other)

    early = projected_rows(
        counts, gate, up, grads, inputs, down_in_proj.T, down_out_proj.T, up_in_proj.T, h
    )
    h_y, h_x, h_y2 = after(h_y, early), after(h_x, early), after(h_y2, early)
    h_xy = swap_x_far(h_y)
    h_yy = swap_y(h_y, 1)
    h_xy2 = swap_y(h_x, 1)
    rows = early + swap_z(early, 0)
    rows_second = swap_z(rows, 1)

    acc = back_step(cols, None, [(h, 0), (h_y, 1), (h_y2, 2), (h_x, 3)], both)
    h_xy = after(h_xy, acc)
    h_xyy = swap_y(h_xy, 1)
    rows = rows + after(rows_second, acc)
    rows = rows + swap_x(rows, 0)
    rows_other = swap_core(rows)
    acc = back_step(cols, acc, [(h_yy, 4), (h_xy2, 5), (h_xy, 6)], both)
    tail = (gate, gate_other, up_out_proj.T, after(rows, acc), rows_other, None)
    second = back_step(cols, acc, [(h_xyy, 7)], both, tail, 0)

    second_other = swap_core(second)
    mine = lax.dynamic_slice_in_dim(second + second_other, core * 16, 16, 1)
    mine = mine + swap_z(mine, 0)
    mine = mine + swap_z(mine, 1)
    mine = mine + swap_x(mine, 0)

    first = rows[:, tokens:].reshape(ex_dev, 32, 128)
    first_other = rows_other[:, tokens:].reshape(ex_dev, 32, 128)
    first_all = jnp.where(is_even, jnp.concatenate([first, first_other]), jnp.concatenate([first_other, first]))
    first_half = lax.dynamic_slice_in_dim(first_all, core * 16, 16, 1)
    ids = jnp.where(is_even, jnp.concatenate([assignment, ids_other]), jnp.concatenate([ids_other, assignment]))
    ids_block = jnp.broadcast_to(jnp.pad(ids, (0, 12))[None, :, None], (1, 16, 128)).astype(BF16)
    load = jnp.concatenate([first_half.astype(BF16), mine.astype(BF16), ids_block])
    load = jnp.stack([load, swap_y(load, 0)])
    load = jnp.concatenate([load, swap_y(load, 1)])
    load = jnp.concatenate([load, swap_x(load, 1)])

    mine_other = swap_core(mine)
    own = lax.dynamic_slice_in_dim(mine, core * ex_dev, ex_dev, 0)
    own_other = lax.dynamic_slice_in_dim(mine_other, core * ex_dev, ex_dev, 0)
    own_rows = jnp.where(is_even, jnp.concatenate([own, own_other], 1), jnp.concatenate([own_other, own], 1))
    out = jnp.stack([first, own_rows]).reshape(2, ex_dev, 32, 2, 64)
    projected = out.transpose(0, 1, 3, 2, 4).reshape(2, ex_dev, 4096)

    flat = load[:, :8].reshape(8, 2, 4, 2048).transpose(1, 0, 2, 3).reshape(2, 32, 2048)
    partial = jnp.einsum("mak,mbk->mab", flat, flat, preferred_element_type=F32)
    slot_ids = load[:, 8, :4, 0].reshape(32).astype(jnp.int32)
    labels = jnp.arange(32, dtype=jnp.int32)
    placing = (slot_ids[None, :] == labels[:, None]).astype(F32)
    by_id = jnp.einsum("as,mst,bt->mab", placing, partial, placing, precision=HIGHEST)
    gram = (by_id + swap_core(by_id)) / 4096.0
    norm = jnp.sqrt(jnp.diagonal(gram, axis1=1, axis2=2) + 1e-06)
    picking = (queries[:, None] == labels[None, :]).astype(F32)
    chosen = jnp.einsum("qa,mab->mqb", picking, gram, precision=HIGHEST)
    chosen_norm = jnp.einsum("qa,ma->mq", picking, norm, precision=HIGHEST)
    scores = chosen / (chosen_norm[:, :, None] * norm[:, None, :])
    return projected, gram, scores


def solution(mesh):
    return jax.shard_map(
        body,
        mesh=mesh,
        in_specs=(
            P("dp", None, "tensor"),
            P("dp", None, "tensor"),
            P("dp", None, "tensor"),
            P("dp", None, None),
            P("tensor", "dp"),
            P("tensor", None),
            P(),
            P("tensor", None),
            P("tensor", None),
            P("dp"),
            P("dp"),
            P(),
        ),
        out_specs=(P(None, "dp", None), P(), P()),
        check_vma=False,
    )
```

```python
import functools

import jax
import jax.numpy as jnp
from jax import lax
from jax.experimental import pallas as pl
from jax.experimental.pallas import tpu as pltpu
from jax.sharding import PartitionSpec as P

AXES = ("dp", "tensor")
BF16, F32 = jnp.bfloat16, jnp.float32
HIGHEST = lax.Precision.HIGHEST
TILE = 512
EARLY_TILE = 256
NT = (((1,), (1,)), ((), ()))
CHUNKS = ((0, 896),)
VMEM_LIMIT = 62 * 2**20
LONG = pl.CostEstimate(flops=10**11, bytes_accessed=10**8, transcendentals=0)


def coords(i):
    dp, tensor = divmod(i, 8)
    x_hi, rest = divmod(dp, 8)
    y, core = divmod(rest, 2)
    x_lo, z = divmod(tensor, 4)
    return x_hi * 2 + x_lo, y, z, core


def index(x, y, z, core):
    x_hi, x_lo = divmod(x % 4, 2)
    return ((x_hi * 4 + y % 4) * 2 + core) * 8 + x_lo * 4 + z % 4


def pair(v, phase):
    return (v ^ 1) if phase == 0 else (v + (1 if v % 2 else -1)) % 4


def moved(value, to):
    return lax.ppermute(value, AXES, [(i, index(*to(*coords(i)))) for i in range(128)])


def swap_core(v):
    return moved(v, lambda x, y, z, c: (x, y, z, 1 - c))


def swap_y(v, step):
    return moved(v, lambda x, y, z, c: (x, pair(y, step ^ c), z, c))


def swap_z(v, step):
    return moved(v, lambda x, y, z, c: (x, y, pair(z, step ^ c), c))


def swap_x(v, phase):
    return moved(v, lambda x, y, z, c: (pair(x, phase), y, z, c))


def swap_x_far(v):
    return moved(v, lambda x, y, z, c: (x + 2, y, z, c))


def silu(v):
    half = 0.5 * v
    return half + half * jnp.tanh(half)


def outer(left, right):
    left_hi, right_hi = left.astype(BF16), right.astype(BF16)
    left_lo = (left - left_hi.astype(F32)).astype(BF16)
    right_lo = (right - right_hi.astype(F32)).astype(BF16)
    sides = jnp.concatenate([left_hi, left_lo], axis=0), jnp.concatenate([right_hi, right_lo], axis=1)
    all_four = jnp.dot(*sides, preferred_element_type=F32)
    n, m = left.shape[0], right.shape[1]
    return all_four[:n, :m] + (all_four[:n, m:] + all_four[n:, :m]) + all_four[n:, m:]


def after(value, *others):
    def nothing(*refs):
        pass

    anywhere = pl.BlockSpec(memory_space=pl.ANY)
    return pl.pallas_call(
        nothing,
        out_shape=jax.ShapeDtypeStruct(value.shape, value.dtype),
        in_specs=[anywhere] * (1 + len(others)),
        out_specs=anywhere,
        input_output_aliases={0: 0},
        name="after",
    )(value, *others)


def rows_kernel(counts, gate, up, grad, inp, din_t, dout_t, uin_t, _, out):
    i = pl.program_id(0)
    per = 512 // EARLY_TILE
    act = silu(gate[...].astype(F32))
    hidden = (act * up[...].astype(F32)).astype(BF16)
    hid_t = lax.dot_general(din_t[...], hidden, NT, preferred_element_type=F32)
    in_t = lax.dot_general(uin_t[...], inp[...], NT, preferred_element_type=F32)
    out_rows = lax.dot_general(grad[...], dout_t[...], NT, preferred_element_type=F32)
    pos = (i % per) * EARLY_TILE + lax.broadcasted_iota(jnp.int32, (64, EARLY_TILE), 1)
    live = (pos < counts[i // per]).astype(F32)
    first = outer(hid_t * live, out_rows)
    packed = jnp.concatenate([first[:32], first[32:]], axis=1)
    here = pl.ds(pl.multiple_of((i // per) * 32, 32), 32)

    @pl.when(i % per == 0)
    def _():
        out[here, 1024:] = packed

    @pl.when(i % per != 0)
    def _():
        out[here, 1024:] += packed

    out[:, pl.ds(pl.multiple_of(i * EARLY_TILE, EARLY_TILE), EARLY_TILE)] = in_t * live


def projected_rows(counts, gate, up, grad, inp, din_t, dout_t, uin_t, later_than):
    tokens, width = gate.shape
    row = lambda n: pl.BlockSpec((EARLY_TILE, n), lambda i, s: (i, 0))
    full = lambda a: pl.BlockSpec(a.shape, lambda i, s: (0, 0))
    return pl.pallas_call(
        rows_kernel,
        out_shape=jax.ShapeDtypeStruct((64, tokens + 128), F32),
        grid_spec=pltpu.PrefetchScalarGridSpec(
            num_scalar_prefetch=1,
            grid=(tokens // EARLY_TILE,),
            in_specs=[row(width), row(width), row(grad.shape[1]), row(inp.shape[1]), full(din_t), full(dout_t), full(uin_t), pl.BlockSpec(memory_space=pl.ANY)],
            out_specs=pl.BlockSpec((64, tokens + 128), lambda i, s: (0, 0)),
        ),
        compiler_params=pltpu.CompilerParams(vmem_limit_bytes=VMEM_LIMIT),
        cost_estimate=LONG,
        name="early_rows",
    )(counts, gate, up, grad, inp, din_t, dout_t, uin_t, later_than)


def back_kernel(n, has_acc, last, has_first, lo, later, cols, *refs):
    i = pl.program_id(0)
    half = pl.num_programs(0) // 2
    refs = list(refs)
    acc_ref = refs.pop(0) if has_acc else None
    refs = refs[:len(refs) - 1 - later] + refs[-1:]
    blocks, rest = refs[: 3 * n], refs[3 * n :]
    out = rest[-1]

    def run(side):
        acc = acc_ref[...] if has_acc else None
        for p in range(n):
            term = lax.dot_general(blocks[3 * p + side][...], blocks[3 * p + 2][...], NT, preferred_element_type=F32)
            acc = term if acc is None else acc + term
        if not last:
            out[...] = acc
            return
        width = acc.shape[1]
        gate = rest[side][:, lo : lo + width]
        delta = (acc * silu(gate.astype(F32))).astype(BF16)
        del_rows = lax.dot_general(delta, rest[2][:, lo : lo + width], NT, preferred_element_type=F32)
        second = outer(rest[3 + side][...], del_rows)
        packed = jnp.concatenate([second[:32], second[32:]], axis=1)

        @pl.when(i % (512 // TILE) == 0)
        def _():
            out[0] = packed + rest[5][0] if has_first else packed

        @pl.when(i % (512 // TILE) != 0)
        def _():
            out[0] += packed

    @pl.when(i < half)
    def _():
        run(0)

    @pl.when(i >= half)
    def _():
        run(1)


def back_step(cols, acc, pieces, grads, tail=None, lo=0, later=()):
    mine, theirs = grads
    tokens = mine.shape[0]
    steps = tokens // TILE
    width = pieces[0][0].shape[0]
    feats = pieces[0][0].shape[1]
    own_row = lambda i: jnp.minimum(i, steps - 1)
    other_row = lambda i: jnp.maximum(i - steps, 0)
    args, specs = [], []
    acc_spec = pl.BlockSpec((TILE, width), lambda i, s: (i, 0))
    if acc is not None:
        args.append(acc)
        specs.append(acc_spec)
    for weight, k in pieces:
        args += [mine, theirs, weight]
        specs += [
            pl.BlockSpec((TILE, feats), lambda i, s, k=k: (own_row(i), s[k])),
            pl.BlockSpec((TILE, feats), lambda i, s, k=k: (other_row(i), s[k])),
            pl.BlockSpec((width, feats), lambda i, s: (0, 0)),
        ]
    n = len(pieces)
    if tail is None:
        out_shape = jax.ShapeDtypeStruct((2 * tokens, width), F32)
        out_spec = acc_spec
    else:
        gate_mine, gate_theirs, proj, rows_mine, rows_theirs, first = tail
        hid = gate_mine.shape[1] // 2
        args += [gate_mine, gate_theirs, proj, rows_mine, rows_theirs]
        specs += [
            pl.BlockSpec((TILE, hid), lambda i, s: (own_row(i), s[8])),
            pl.BlockSpec((TILE, hid), lambda i, s: (other_row(i), s[8])),
            pl.BlockSpec((64, hid), lambda i, s: (0, s[8])),
            pl.BlockSpec((64, TILE), lambda i, s: (0, own_row(i))),
            pl.BlockSpec((64, TILE), lambda i, s: (0, other_row(i))),
        ]
        out_spec = pl.BlockSpec((1, 32, 128), lambda i, s: ((i // (512 // TILE) + 2 * s[8]) % 4, 0, 0))
        if first is not None:
            args.append(first)
            specs.append(out_spec)
        out_shape = jax.ShapeDtypeStruct((4, 32, 128), F32)
    args += later
    specs += [pl.BlockSpec(memory_space=pl.ANY)] * len(later)
    return pl.pallas_call(
        functools.partial(back_kernel, n, acc is not None, tail is not None, tail is not None and tail[5] is not None, lo, len(later)),
        out_shape=out_shape,
        grid_spec=pltpu.PrefetchScalarGridSpec(
            num_scalar_prefetch=1, grid=(2 * steps,), in_specs=specs, out_specs=out_spec
        ),
        compiler_params=pltpu.CompilerParams(vmem_limit_bytes=VMEM_LIMIT),
        cost_estimate=LONG,
        name="back_last" if tail is not None else "back_part",
    )(cols, *args)


def body(
    gate_pre, up_val, layer_in, out_grad, down_weight, down_in_proj, down_out_proj,
    up_in_proj, up_out_proj, counts, assignment, queries,
):
    ex_dev, seq_len, width_ff = gate_pre.shape
    tokens = ex_dev * seq_len
    half = width_ff // 2
    dp = lax.axis_index("dp")
    core = dp % 2
    y = (dp // 2) % 4
    x_hi = dp // 8

    def partner(v, step):
        odd = (step ^ core) == 0
        return jnp.where(odd, v ^ 1, (v + jnp.where(v % 2 == 1, 1, 3)) % 4)

    y1, y2 = partner(y, 0), partner(y, 1)
    y12 = partner(y2, 0)
    here, there = x_hi * 4, (1 - x_hi) * 4
    cols = jnp.stack(
        [here + y, here + y1, here + y2, there + y, here + y12, there + y2, there + y1, there + y12, core]
    ).astype(jnp.int32)

    gate = gate_pre.reshape(tokens, width_ff)
    up = up_val.reshape(tokens, width_ff)
    grads = out_grad.reshape(tokens, -1)
    inputs = layer_in.reshape(tokens, -1)

    weight_other = swap_core(down_weight)
    ids_other = swap_core(assignment)
    is_even = core == 0
    even = jnp.concatenate([down_weight[:half], weight_other[:half]], axis=1)
    odd = jnp.concatenate([weight_other[half:], down_weight[half:]], axis=1)
    h = jnp.where(is_even, even, odd)

    h_x = swap_x_far(h)
    h_y = swap_y(h, 0)
    h_y2 = swap_y(h, 1)
    early = projected_rows(
        counts, gate, up, grads, inputs, down_in_proj.T, down_out_proj.T, up_in_proj.T, h
    )
    grads_other = swap_core(grads)
    gate_other = swap_core(gate)
    both = (grads, grads_other)
    h_y, h_x, h_y2 = after(h_y, early), after(h_x, early), after(h_y2, early)
    h_xy = swap_x_far(h_y)
    h_yy = swap_y(h_y, 1)
    h_xy2 = swap_y(h_x, 1)
    rows = early + swap_z(early, 0)
    rows_second = swap_z(rows, 1)
    acc = back_step(cols, None, [(h, 0), (h_y, 1), (h_y2, 2), (h_x, 3)], both, later=(rows,))

    h_xy = after(h_xy, acc)
    h_xyy = swap_y(h_xy, 1)
    rows = rows + after(rows_second, acc)
    rows_third = swap_x(rows, 0)
    acc = back_step(cols, acc, [(h_yy, 4), (h_xy2, 5), (h_xy, 6)], both, later=(rows,))
    rows = rows + after(rows_third, acc)
    rows_other = swap_core(rows)
    tail = (gate, gate_other, up_out_proj.T, rows, rows_other, None)
    second = back_step(cols, acc, [(h_xyy, 7)], both, tail, 0)

    second_other = swap_core(second)
    mine = lax.dynamic_slice_in_dim(second + second_other, core * 16, 16, 1)
    mine = mine + swap_z(mine, 0)
    mine = mine + swap_z(mine, 1)
    mine = mine + swap_x(mine, 0)

    first = rows[:, tokens:].reshape(ex_dev, 32, 128)
    first_other = rows_other[:, tokens:].reshape(ex_dev, 32, 128)
    first_all = jnp.where(is_even, jnp.concatenate([first, first_other]), jnp.concatenate([first_other, first]))
    first_half = lax.dynamic_slice_in_dim(first_all, core * 16, 16, 1)
    ids = jnp.where(is_even, jnp.concatenate([assignment, ids_other]), jnp.concatenate([ids_other, assignment]))
    ids_block = jnp.broadcast_to(jnp.pad(ids, (0, 12))[None, :, None], (1, 16, 128)).astype(BF16)
    load = jnp.concatenate([first_half.astype(BF16), mine.astype(BF16), ids_block])
    load = jnp.stack([load, swap_y(load, 0)])
    load = jnp.concatenate([load, swap_y(load, 1)])
    load = jnp.concatenate([load, swap_x(load, 1)])

    mine_other = swap_core(mine)
    own = lax.dynamic_slice_in_dim(mine, core * ex_dev, ex_dev, 0)
    own_other = lax.dynamic_slice_in_dim(mine_other, core * ex_dev, ex_dev, 0)
    own_rows = jnp.where(is_even, jnp.concatenate([own, own_other], 1), jnp.concatenate([own_other, own], 1))
    out = jnp.stack([first, own_rows]).reshape(2, ex_dev, 32, 2, 64)
    projected = out.transpose(0, 1, 3, 2, 4).reshape(2, ex_dev, 4096)

    flat = load[:, :8].reshape(8, 2, 4, 2048).transpose(1, 0, 2, 3).reshape(2, 32, 2048)
    partial = jnp.einsum("mak,mbk->mab", flat, flat, preferred_element_type=F32)
    slot_ids = load[:, 8, :4, 0].reshape(32).astype(jnp.int32)
    labels = jnp.arange(32, dtype=jnp.int32)
    placing = (slot_ids[None, :] == labels[:, None]).astype(F32)
    by_id = jnp.einsum("as,mst,bt->mab", placing, partial, placing, precision=HIGHEST)
    gram = (by_id + swap_core(by_id)) / 4096.0
    norm = jnp.sqrt(jnp.sum(gram * jnp.eye(32, dtype=F32), axis=2) + 1e-06)
    picking = (queries[:, None] == labels[None, :]).astype(F32)
    chosen = jnp.einsum("qa,mab->mqb", picking, gram, precision=HIGHEST)
    chosen_norm = jnp.einsum("qa,ma->mq", picking, norm, precision=HIGHEST)
    scores = chosen / (chosen_norm[:, :, None] * norm[:, None, :])
    return projected, gram, scores


def solution(mesh):
    return jax.shard_map(
        body,
        mesh=mesh,
        in_specs=(
            P("dp", None, "tensor"),
            P("dp", None, "tensor"),
            P("dp", None, "tensor"),
            P("dp", None, None),
            P("tensor", "dp"),
            P("tensor", None),
            P(),
            P("tensor", None),
            P("tensor", None),
            P("dp"),
            P("dp"),
            P(),
        ),
        out_specs=(P(None, "dp", None), P(), P()),
        check_vma=False,
    )
```

```python
import functools

import jax
import jax.numpy as jnp
from jax import lax
from jax.experimental import pallas as pl
from jax.experimental.pallas import tpu as pltpu
from jax.sharding import PartitionSpec as P

AXES = ("dp", "tensor")
BF16, F32 = jnp.bfloat16, jnp.float32
HIGHEST = lax.Precision.HIGHEST
TILE = 512
EARLY_TILE = 256
NT = (((1,), (1,)), ((), ()))
CHUNKS = ((0, 896),)
VMEM_LIMIT = 62 * 2**20
LONG = pl.CostEstimate(flops=10**11, bytes_accessed=10**8, transcendentals=0)


def coords(i):
    dp, tensor = divmod(i, 8)
    x_hi, rest = divmod(dp, 8)
    y, core = divmod(rest, 2)
    x_lo, z = divmod(tensor, 4)
    return x_hi * 2 + x_lo, y, z, core


def index(x, y, z, core):
    x_hi, x_lo = divmod(x % 4, 2)
    return ((x_hi * 4 + y % 4) * 2 + core) * 8 + x_lo * 4 + z % 4


def pair(v, phase):
    return (v ^ 1) if phase == 0 else (v + (1 if v % 2 else -1)) % 4


def moved(value, to):
    return lax.ppermute(value, AXES, [(i, index(*to(*coords(i)))) for i in range(128)])


def swap_core(v):
    return moved(v, lambda x, y, z, c: (x, y, z, 1 - c))


def swap_y(v, step):
    return moved(v, lambda x, y, z, c: (x, pair(y, step ^ c), z, c))


def swap_z(v, step):
    return moved(v, lambda x, y, z, c: (x, y, pair(z, step ^ c), c))


def swap_x(v, phase):
    return moved(v, lambda x, y, z, c: (pair(x, phase), y, z, c))


def swap_x_far(v):
    return moved(v, lambda x, y, z, c: (x + 2, y, z, c))


def silu(v):
    half = 0.5 * v
    return half + half * jnp.tanh(half)


def outer(left, right):
    left_hi, right_hi = left.astype(BF16), right.astype(BF16)
    left_lo = (left - left_hi.astype(F32)).astype(BF16)
    right_lo = (right - right_hi.astype(F32)).astype(BF16)
    sides = jnp.concatenate([left_hi, left_lo], axis=0), jnp.concatenate([right_hi, right_lo], axis=1)
    all_four = jnp.dot(*sides, preferred_element_type=F32)
    n, m = left.shape[0], right.shape[1]
    return all_four[:n, :m] + (all_four[:n, m:] + all_four[n:, :m]) + all_four[n:, m:]


def after(value, *others):
    def nothing(*refs):
        pass

    anywhere = pl.BlockSpec(memory_space=pl.ANY)
    return pl.pallas_call(
        nothing,
        out_shape=jax.ShapeDtypeStruct(value.shape, value.dtype),
        in_specs=[anywhere] * (1 + len(others)),
        out_specs=anywhere,
        input_output_aliases={0: 0},
        name="after",
    )(value, *others)


def rows_kernel(counts, gate, up, grad, inp, din_t, dout_t, uin_t, _, out):
    i = pl.program_id(0)
    per = 512 // EARLY_TILE
    act = silu(gate[...].astype(F32))
    hidden = (act * up[...].astype(F32)).astype(BF16)
    hid_t = lax.dot_general(din_t[...], hidden, NT, preferred_element_type=F32)
    in_t = lax.dot_general(uin_t[...], inp[...], NT, preferred_element_type=F32)
    out_rows = lax.dot_general(grad[...], dout_t[...], NT, preferred_element_type=F32)
    pos = (i % per) * EARLY_TILE + lax.broadcasted_iota(jnp.int32, (64, EARLY_TILE), 1)
    live = (pos < counts[i // per]).astype(F32)
    first = outer(hid_t * live, out_rows)
    packed = jnp.concatenate([first[:32], first[32:]], axis=1)
    here = pl.ds(pl.multiple_of((i // per) * 32, 32), 32)

    @pl.when(i % per == 0)
    def _():
        out[here, 1024:] = packed

    @pl.when(i % per != 0)
    def _():
        out[here, 1024:] += packed

    out[:, pl.ds(pl.multiple_of(i * EARLY_TILE, EARLY_TILE), EARLY_TILE)] = in_t * live


def projected_rows(counts, gate, up, grad, inp, din_t, dout_t, uin_t, later_than):
    tokens, width = gate.shape
    row = lambda n: pl.BlockSpec((EARLY_TILE, n), lambda i, s: (i, 0))
    full = lambda a: pl.BlockSpec(a.shape, lambda i, s: (0, 0))
    return pl.pallas_call(
        rows_kernel,
        out_shape=jax.ShapeDtypeStruct((64, tokens + 128), F32),
        grid_spec=pltpu.PrefetchScalarGridSpec(
            num_scalar_prefetch=1,
            grid=(tokens // EARLY_TILE,),
            in_specs=[row(width), row(width), row(grad.shape[1]), row(inp.shape[1]), full(din_t), full(dout_t), full(uin_t), pl.BlockSpec(memory_space=pl.ANY)],
            out_specs=pl.BlockSpec((64, tokens + 128), lambda i, s: (0, 0)),
        ),
        compiler_params=pltpu.CompilerParams(vmem_limit_bytes=VMEM_LIMIT),
        cost_estimate=LONG,
        name="early_rows",
    )(counts, gate, up, grad, inp, din_t, dout_t, uin_t, later_than)


def back_kernel(n, has_acc, last, lo, later, cols, *refs):
    i = pl.program_id(0)
    half = pl.num_programs(0) // 2
    refs = list(refs)
    acc_ref = refs.pop(0) if has_acc else None
    refs = refs[:len(refs) - 1 - later] + refs[-1:]
    blocks, rest = refs[: 3 * n], refs[3 * n :]
    out = rest[-1]

    def run(side):
        acc = acc_ref[...] if has_acc else None
        for p in range(n):
            term = lax.dot_general(blocks[3 * p + side][...], blocks[3 * p + 2][...], NT, preferred_element_type=F32)
            acc = term if acc is None else acc + term
        if not last:
            out[...] = acc
            return
        width = acc.shape[1]
        gate = rest[side][:, lo : lo + width]
        delta = (acc * silu(gate.astype(F32))).astype(BF16)
        del_rows = lax.dot_general(delta, rest[2][:, lo : lo + width], NT, preferred_element_type=F32)
        second = outer(rest[3 + 2 * side][...] + rest[4 + 2 * side][...], del_rows)
        packed = jnp.concatenate([second[:32], second[32:]], axis=1)

        @pl.when(i % (512 // TILE) == 0)
        def _():
            out[0] = packed

        @pl.when(i % (512 // TILE) != 0)
        def _():
            out[0] += packed

    @pl.when(i < half)
    def _():
        run(0)

    @pl.when(i >= half)
    def _():
        run(1)


def back_step(cols, acc, pieces, grads, tail=None, lo=0, later=()):
    mine, theirs = grads
    tokens = mine.shape[0]
    steps = tokens // TILE
    width = pieces[0][0].shape[0]
    feats = pieces[0][0].shape[1]
    own_row = lambda i: jnp.minimum(i, steps - 1)
    other_row = lambda i: jnp.maximum(i - steps, 0)
    args, specs = [], []
    acc_spec = pl.BlockSpec((TILE, width), lambda i, s: (i, 0))
    if acc is not None:
        args.append(acc)
        specs.append(acc_spec)
    for weight, k in pieces:
        args += [mine, theirs, weight]
        specs += [
            pl.BlockSpec((TILE, feats), lambda i, s, k=k: (own_row(i), s[k])),
            pl.BlockSpec((TILE, feats), lambda i, s, k=k: (other_row(i), s[k])),
            pl.BlockSpec((width, feats), lambda i, s: (0, 0)),
        ]
    n = len(pieces)
    if tail is None:
        out_shape = jax.ShapeDtypeStruct((2 * tokens, width), F32)
        out_spec = acc_spec
    else:
        hid = tail[0].shape[1] // 2
        args += tail
        mine_rows = pl.BlockSpec((64, TILE), lambda i, s: (0, own_row(i)))
        their_rows = pl.BlockSpec((64, TILE), lambda i, s: (0, other_row(i)))
        specs += [
            pl.BlockSpec((TILE, hid), lambda i, s: (own_row(i), s[8])),
            pl.BlockSpec((TILE, hid), lambda i, s: (other_row(i), s[8])),
            pl.BlockSpec((64, hid), lambda i, s: (0, s[8])),
            mine_rows,
            mine_rows,
            their_rows,
            their_rows,
        ]
        out_spec = pl.BlockSpec((1, 32, 128), lambda i, s: ((i // (512 // TILE) + 2 * s[8]) % 4, 0, 0))
        out_shape = jax.ShapeDtypeStruct((4, 32, 128), F32)
    args += later
    specs += [pl.BlockSpec(memory_space=pl.ANY)] * len(later)
    return pl.pallas_call(
        functools.partial(back_kernel, n, acc is not None, tail is not None, lo, len(later)),
        out_shape=out_shape,
        grid_spec=pltpu.PrefetchScalarGridSpec(
            num_scalar_prefetch=1, grid=(2 * steps,), in_specs=specs, out_specs=out_spec
        ),
        compiler_params=pltpu.CompilerParams(vmem_limit_bytes=VMEM_LIMIT),
        cost_estimate=LONG,
        name="back_last" if tail is not None else "back_part",
    )(cols, *args)


def body(
    gate_pre, up_val, layer_in, out_grad, down_weight, down_in_proj, down_out_proj,
    up_in_proj, up_out_proj, counts, assignment, queries,
):
    ex_dev, seq_len, width_ff = gate_pre.shape
    tokens = ex_dev * seq_len
    half = width_ff // 2
    dp = lax.axis_index("dp")
    core = dp % 2
    y = (dp // 2) % 4
    x_hi = dp // 8

    def partner(v, step):
        odd = (step ^ core) == 0
        return jnp.where(odd, v ^ 1, (v + jnp.where(v % 2 == 1, 1, 3)) % 4)

    y1, y2 = partner(y, 0), partner(y, 1)
    y12 = partner(y2, 0)
    here, there = x_hi * 4, (1 - x_hi) * 4
    cols = jnp.stack(
        [here + y, here + y1, here + y2, there + y, here + y12, there + y2, there + y1, there + y12, core]
    ).astype(jnp.int32)

    gate = gate_pre.reshape(tokens, width_ff)
    up = up_val.reshape(tokens, width_ff)
    grads = out_grad.reshape(tokens, -1)
    inputs = layer_in.reshape(tokens, -1)

    weight_other = swap_core(down_weight)
    ids_other = swap_core(assignment)
    is_even = core == 0
    even = jnp.concatenate([down_weight[:half], weight_other[:half]], axis=1)
    odd = jnp.concatenate([weight_other[half:], down_weight[half:]], axis=1)
    h = jnp.where(is_even, even, odd)

    h_x = swap_x_far(h)
    h_y = swap_y(h, 0)
    h_y2 = swap_y(h, 1)
    early = projected_rows(
        counts, gate, up, grads, inputs, down_in_proj.T, down_out_proj.T, up_in_proj.T, h
    )
    grads_other = swap_core(grads)
    gate_other = swap_core(gate)
    both = (grads, grads_other)
    h_y, h_x, h_y2 = after(h_y, early), after(h_x, early), after(h_y2, early)
    h_xy = swap_x_far(h_y)
    h_yy = swap_y(h_y, 1)
    h_xy2 = swap_y(h_x, 1)
    rows = early + swap_z(early, 0)
    rows_second = swap_z(rows, 1)
    acc = back_step(cols, None, [(h, 0), (h_y, 1), (h_y2, 2), (h_x, 3)], both, later=(rows,))

    h_xy = after(h_xy, acc)
    h_xyy = swap_y(h_xy, 1)
    rows = rows + after(rows_second, acc)
    rows_x = swap_x(rows, 0)
    rows_core = swap_core(rows)
    rows_x_core = moved(rows, lambda x, y, z, c: (pair(x, 0), y, z, 1 - c))
    acc = back_step(cols, acc, [(h_yy, 4), (h_xy2, 5), (h_xy, 6)], both, later=(rows,))
    tail = (gate, gate_other, up_out_proj.T, rows, rows_x, rows_core, rows_x_core)
    second = back_step(cols, acc, [(h_xyy, 7)], both, tail, 0)

    second_other = swap_core(second)
    mine = lax.dynamic_slice_in_dim(second + second_other, core * 16, 16, 1)
    mine = mine + swap_z(mine, 0)
    mine = mine + swap_z(mine, 1)
    mine = mine + swap_x(mine, 0)

    first = (rows[:, tokens:] + rows_x[:, tokens:]).reshape(ex_dev, 32, 128)
    first_other = (rows_core[:, tokens:] + rows_x_core[:, tokens:]).reshape(ex_dev, 32, 128)
    first_all = jnp.where(is_even, jnp.concatenate([first, first_other]), jnp.concatenate([first_other, first]))
    first_half = lax.dynamic_slice_in_dim(first_all, core * 16, 16, 1)
    ids = jnp.where(is_even, jnp.concatenate([assignment, ids_other]), jnp.concatenate([ids_other, assignment]))
    ids_block = jnp.broadcast_to(jnp.pad(ids, (0, 12))[None, :, None], (1, 16, 128)).astype(BF16)
    load = jnp.concatenate([first_half.astype(BF16), mine.astype(BF16), ids_block])
    load = jnp.stack([load, swap_x(load, 1)])
    load = jnp.concatenate([load, swap_y(load, 0)])
    load = jnp.concatenate([load, swap_y(load, 1)])

    mine_other = swap_core(mine)
    own = lax.dynamic_slice_in_dim(mine, core * ex_dev, ex_dev, 0)
    own_other = lax.dynamic_slice_in_dim(mine_other, core * ex_dev, ex_dev, 0)
    own_rows = jnp.where(is_even, jnp.concatenate([own, own_other], 1), jnp.concatenate([own_other, own], 1))
    out = jnp.stack([first, own_rows]).reshape(2, ex_dev, 32, 2, 64)
    projected = out.transpose(0, 1, 3, 2, 4).reshape(2, ex_dev, 4096)

    flat = load[:, :8].reshape(8, 2, 4, 2048).transpose(1, 0, 2, 3).reshape(2, 32, 2048)
    partial = jnp.einsum("mak,mbk->mab", flat, flat, preferred_element_type=F32)
    slot_ids = load[:, 8, :4, 0].reshape(32).astype(jnp.int32)
    labels = jnp.arange(32, dtype=jnp.int32)
    placing = (slot_ids[None, :] == labels[:, None]).astype(F32)
    by_id = jnp.einsum("as,mst,bt->mab", placing, partial, placing, precision=HIGHEST)
    gram = (by_id + swap_core(by_id)) / 4096.0
    norm = jnp.sqrt(jnp.sum(gram * jnp.eye(32, dtype=F32), axis=2) + 1e-06)
    picking = (queries[:, None] == labels[None, :]).astype(F32)
    chosen = jnp.einsum("qa,mab->mqb", picking, gram, precision=HIGHEST)
    chosen_norm = jnp.einsum("qa,ma->mq", picking, norm, precision=HIGHEST)
    scores = chosen / (chosen_norm[:, :, None] * norm[:, None, :])
    return projected, gram, scores


def solution(mesh):
    return jax.shard_map(
        body,
        mesh=mesh,
        in_specs=(
            P("dp", None, "tensor"),
            P("dp", None, "tensor"),
            P("dp", None, "tensor"),
            P("dp", None, None),
            P("tensor", "dp"),
            P("tensor", None),
            P(),
            P("tensor", None),
            P("tensor", None),
            P("dp"),
            P("dp"),
            P(),
        ),
        out_specs=(P(None, "dp", None), P(), P()),
        check_vma=False,
    )
```

```python
import functools

import jax
import jax.numpy as jnp
from jax import lax
from jax.experimental import pallas as pl
from jax.experimental.pallas import tpu as pltpu
from jax.sharding import PartitionSpec as P

AXES = ("dp", "tensor")
BF16, F32 = jnp.bfloat16, jnp.float32
HIGHEST = lax.Precision.HIGHEST
TILE = 512
EARLY_TILE = 256
NT = (((1,), (1,)), ((), ()))
CHUNKS = ((0, 896),)
VMEM_LIMIT = 60 * 2**20
BACK_LIMIT = 50 * 2**20
LONG = pl.CostEstimate(flops=10**11, bytes_accessed=10**8, transcendentals=0)


def coords(i):
    dp, tensor = divmod(i, 8)
    x_hi, rest = divmod(dp, 8)
    y, core = divmod(rest, 2)
    x_lo, z = divmod(tensor, 4)
    return x_hi * 2 + x_lo, y, z, core


def index(x, y, z, core):
    x_hi, x_lo = divmod(x % 4, 2)
    return ((x_hi * 4 + y % 4) * 2 + core) * 8 + x_lo * 4 + z % 4


def pair(v, phase):
    return (v ^ 1) if phase == 0 else (v + (1 if v % 2 else -1)) % 4


def moved(value, to):
    return lax.ppermute(value, AXES, [(i, index(*to(*coords(i)))) for i in range(128)])


def swap_core(v):
    return moved(v, lambda x, y, z, c: (x, y, z, 1 - c))


def swap_y(v, step):
    return moved(v, lambda x, y, z, c: (x, pair(y, step ^ c), z, c))


def swap_z(v, step):
    return moved(v, lambda x, y, z, c: (x, y, pair(z, step ^ c), c))


def swap_x(v, phase):
    return moved(v, lambda x, y, z, c: (pair(x, phase), y, z, c))


def swap_x_far(v):
    return moved(v, lambda x, y, z, c: (x + 2, y, z, c))


def silu(v):
    half = 0.5 * v
    return half + half * jnp.tanh(half)


def outer(left, right):
    left_hi, right_hi = left.astype(BF16), right.astype(BF16)
    left_lo = (left - left_hi.astype(F32)).astype(BF16)
    right_lo = (right - right_hi.astype(F32)).astype(BF16)
    sides = jnp.concatenate([left_hi, left_lo], axis=0), jnp.concatenate([right_hi, right_lo], axis=1)
    all_four = jnp.dot(*sides, preferred_element_type=F32)
    n, m = left.shape[0], right.shape[1]
    return all_four[:n, :m] + (all_four[:n, m:] + all_four[n:, :m]) + all_four[n:, m:]


def after(value, *others):
    def nothing(*refs):
        pass

    anywhere = pl.BlockSpec(memory_space=pl.ANY)
    return pl.pallas_call(
        nothing,
        out_shape=jax.ShapeDtypeStruct(value.shape, value.dtype),
        in_specs=[anywhere] * (1 + len(others)),
        out_specs=anywhere,
        input_output_aliases={0: 0},
        name="after",
    )(value, *others)


def rows_kernel(counts, gate, up, grad, inp, din_t, dout_t, uin_t, _, out):
    i = pl.program_id(0)
    per = 512 // EARLY_TILE
    act = silu(gate[...].astype(F32))
    hidden = (act * up[...].astype(F32)).astype(BF16)
    hid_t = lax.dot_general(din_t[...], hidden, NT, preferred_element_type=F32)
    in_t = lax.dot_general(uin_t[...], inp[...], NT, preferred_element_type=F32)
    out_rows = lax.dot_general(grad[...], dout_t[...], NT, preferred_element_type=F32)
    pos = (i % per) * EARLY_TILE + lax.broadcasted_iota(jnp.int32, (64, EARLY_TILE), 1)
    live = (pos < counts[i // per]).astype(F32)
    first = outer(hid_t * live, out_rows)
    packed = jnp.concatenate([first[:32], first[32:]], axis=1)
    here = pl.ds(pl.multiple_of((i // per) * 32, 32), 32)

    @pl.when(i % per == 0)
    def _():
        out[here, 1024:] = packed

    @pl.when(i % per != 0)
    def _():
        out[here, 1024:] += packed

    out[:, pl.ds(pl.multiple_of(i * EARLY_TILE, EARLY_TILE), EARLY_TILE)] = in_t * live


def projected_rows(counts, gate, up, grad, inp, din_t, dout_t, uin_t, later_than):
    tokens, width = gate.shape
    row = lambda n: pl.BlockSpec((EARLY_TILE, n), lambda i, s: (i, 0))
    full = lambda a: pl.BlockSpec(a.shape, lambda i, s: (0, 0))
    return pl.pallas_call(
        rows_kernel,
        out_shape=jax.ShapeDtypeStruct((64, tokens + 128), F32),
        grid_spec=pltpu.PrefetchScalarGridSpec(
            num_scalar_prefetch=1,
            grid=(tokens // EARLY_TILE,),
            in_specs=[row(width), row(width), row(grad.shape[1]), row(inp.shape[1]), full(din_t), full(dout_t), full(uin_t), pl.BlockSpec(memory_space=pl.ANY)],
            out_specs=pl.BlockSpec((64, tokens + 128), lambda i, s: (0, 0)),
        ),
        compiler_params=pltpu.CompilerParams(vmem_limit_bytes=VMEM_LIMIT),
        cost_estimate=LONG,
        name="early_rows",
    )(counts, gate, up, grad, inp, din_t, dout_t, uin_t, later_than)


def back_kernel(n, has_acc, last, lo, later, cols, *refs):
    i = pl.program_id(0)
    half = pl.num_programs(0) // 2
    refs = list(refs)
    if not last:
        refs.pop()[...] = jnp.zeros((8, 128), F32)
    acc_ref = refs.pop(0) if has_acc else None
    refs = refs[:len(refs) - 1 - later] + refs[-1:]
    blocks, rest = refs[: 3 * n], refs[3 * n :]
    out = rest[-1]

    def run(side):
        acc = acc_ref[...] if has_acc else None
        for p in range(n):
            term = lax.dot_general(blocks[3 * p + side][...], blocks[3 * p + 2][...], NT, preferred_element_type=F32)
            acc = term if acc is None else acc + term
        if not last:
            out[...] = acc
            return
        width = acc.shape[1]
        gate = rest[side][:, lo : lo + width]
        delta = (acc * silu(gate.astype(F32))).astype(BF16)
        del_rows = lax.dot_general(delta, rest[2][:, lo : lo + width], NT, preferred_element_type=F32)
        second = outer(rest[3 + 2 * side][...] + rest[4 + 2 * side][...], del_rows)
        packed = jnp.concatenate([second[:32], second[32:]], axis=1)

        @pl.when(i % (512 // TILE) == 0)
        def _():
            out[0] = packed

        @pl.when(i % (512 // TILE) != 0)
        def _():
            out[0] += packed

    @pl.when(i < half)
    def _():
        run(0)

    @pl.when(i >= half)
    def _():
        run(1)


def back_step(cols, acc, pieces, grads, tail=None, lo=0, later=()):
    mine, theirs = grads
    tokens = mine.shape[0]
    steps = tokens // TILE
    width = pieces[0][0].shape[0]
    feats = pieces[0][0].shape[1]
    own_row = lambda i: jnp.minimum(i, steps - 1)
    other_row = lambda i: jnp.maximum(i - steps, 0)
    args, specs = [], []
    acc_spec = pl.BlockSpec((TILE, width), lambda i, s: (i, 0))
    if acc is not None:
        args.append(acc)
        specs.append(acc_spec)
    for weight, k in pieces:
        args += [mine, theirs, weight]
        specs += [
            pl.BlockSpec((TILE, feats), lambda i, s, k=k: (own_row(i), s[k])),
            pl.BlockSpec((TILE, feats), lambda i, s, k=k: (other_row(i), s[k])),
            pl.BlockSpec((width, feats), lambda i, s: (0, 0)),
        ]
    n = len(pieces)
    if tail is None:
        out_shape = (jax.ShapeDtypeStruct((2 * tokens, width), F32), jax.ShapeDtypeStruct((8, 128), F32))
        out_spec = (acc_spec, pl.BlockSpec((8, 128), lambda i, s: (0, 0)))
    else:
        hid = tail[0].shape[1] // 2
        args += tail
        mine_rows = pl.BlockSpec((64, TILE), lambda i, s: (0, own_row(i)))
        their_rows = pl.BlockSpec((64, TILE), lambda i, s: (0, other_row(i)))
        specs += [
            pl.BlockSpec((TILE, hid), lambda i, s: (own_row(i), s[8])),
            pl.BlockSpec((TILE, hid), lambda i, s: (other_row(i), s[8])),
            pl.BlockSpec((64, hid), lambda i, s: (0, s[8])),
            mine_rows,
            mine_rows,
            their_rows,
            their_rows,
        ]
        out_spec = pl.BlockSpec((1, 32, 128), lambda i, s: ((i // (512 // TILE) + 2 * s[8]) % 4, 0, 0))
        out_shape = jax.ShapeDtypeStruct((4, 32, 128), F32)
    args += later
    specs += [pl.BlockSpec(memory_space=pl.ANY)] * len(later)
    return pl.pallas_call(
        functools.partial(back_kernel, n, acc is not None, tail is not None, lo, len(later)),
        out_shape=out_shape,
        grid_spec=pltpu.PrefetchScalarGridSpec(
            num_scalar_prefetch=1, grid=(2 * steps,), in_specs=specs, out_specs=out_spec
        ),
        input_output_aliases={1: 0} if acc is not None and tail is None else {},
        compiler_params=pltpu.CompilerParams(vmem_limit_bytes=BACK_LIMIT),
        cost_estimate=LONG,
        name="back_last" if tail is not None else "back_part",
    )(cols, *args)


def body(
    gate_pre, up_val, layer_in, out_grad, down_weight, down_in_proj, down_out_proj,
    up_in_proj, up_out_proj, counts, assignment, queries,
):
    ex_dev, seq_len, width_ff = gate_pre.shape
    tokens = ex_dev * seq_len
    half = width_ff // 2
    dp = lax.axis_index("dp")
    core = dp % 2
    y = (dp // 2) % 4
    x_hi = dp // 8

    def partner(v, step):
        odd = (step ^ core) == 0
        return jnp.where(odd, v ^ 1, (v + jnp.where(v % 2 == 1, 1, 3)) % 4)

    y1, y2 = partner(y, 0), partner(y, 1)
    y12 = partner(y2, 0)
    here, there = x_hi * 4, (1 - x_hi) * 4
    cols = jnp.stack(
        [here + y, here + y1, here + y2, there + y, here + y12, there + y2, there + y1, there + y12, core]
    ).astype(jnp.int32)

    gate = gate_pre.reshape(tokens, width_ff)
    up = up_val.reshape(tokens, width_ff)
    grads = out_grad.reshape(tokens, -1)
    inputs = layer_in.reshape(tokens, -1)

    weight_other = swap_core(down_weight)
    ids_other = swap_core(assignment)
    is_even = core == 0
    even = jnp.concatenate([down_weight[:half], weight_other[:half]], axis=1)
    odd = jnp.concatenate([weight_other[half:], down_weight[half:]], axis=1)
    h = jnp.where(is_even, even, odd)

    h_x = swap_x_far(h)
    h_y = swap_y(h, 0)
    h_y2 = swap_y(h, 1)
    early = projected_rows(
        counts, gate, up, grads, inputs, down_in_proj.T, down_out_proj.T, up_in_proj.T, h
    )
    grads_other = swap_core(grads)
    gate_other = swap_core(gate)
    both = (grads, grads_other)
    h_y, h_x, h_y2 = after(h_y, early), after(h_x, early), after(h_y2, early)
    h_xy = swap_x_far(h_y)
    h_yy = swap_y(h_y, 1)
    h_xy2 = swap_y(h_x, 1)
    rows = early + swap_z(early, 0)
    rows_second = swap_z(rows, 1)
    acc, done = back_step(cols, None, [(h, 0), (h_y, 1), (h_y2, 2), (h_x, 3)], both, later=(rows,))

    h_xy = after(h_xy, done)
    h_xyy = swap_y(h_xy, 1)
    rows = rows + after(rows_second, done)
    rows_x = swap_x(rows, 0)
    rows_core = swap_core(rows)
    rows_x_core = moved(rows, lambda x, y, z, c: (pair(x, 0), y, z, 1 - c))
    acc, _ = back_step(cols, acc, [(h_yy, 4), (h_xy2, 5), (h_xy, 6)], both, later=(rows,))
    tail = (gate, gate_other, up_out_proj.T, rows, rows_x, rows_core, rows_x_core)
    second = back_step(cols, acc, [(h_xyy, 7)], both, tail, 0)

    second_other = swap_core(second)
    mine = lax.dynamic_slice_in_dim(second + second_other, core * 16, 16, 1)
    mine = mine + swap_z(mine, 0)
    mine = mine + swap_z(mine, 1)
    mine = mine + swap_x(mine, 0)

    first = (rows[:, tokens:] + rows_x[:, tokens:]).reshape(ex_dev, 32, 128)
    first_other = (rows_core[:, tokens:] + rows_x_core[:, tokens:]).reshape(ex_dev, 32, 128)
    first_all = jnp.where(is_even, jnp.concatenate([first, first_other]), jnp.concatenate([first_other, first]))
    first_half = lax.dynamic_slice_in_dim(first_all, core * 16, 16, 1)
    ids = jnp.where(is_even, jnp.concatenate([assignment, ids_other]), jnp.concatenate([ids_other, assignment]))
    ids_block = jnp.broadcast_to(jnp.pad(ids, (0, 12))[None, :, None], (1, 16, 128)).astype(BF16)
    load = jnp.concatenate([first_half.astype(BF16), mine.astype(BF16), ids_block])
    load = jnp.stack([load, swap_x(load, 1)])
    load = jnp.concatenate([load, swap_y(load, 0)])
    load = jnp.concatenate([load, swap_y(load, 1)])

    mine_other = swap_core(mine)
    own = lax.dynamic_slice_in_dim(mine, core * ex_dev, ex_dev, 0)
    own_other = lax.dynamic_slice_in_dim(mine_other, core * ex_dev, ex_dev, 0)
    own_rows = jnp.where(is_even, jnp.concatenate([own, own_other], 1), jnp.concatenate([own_other, own], 1))
    out = jnp.stack([first, own_rows]).reshape(2, ex_dev, 32, 2, 64)
    projected = out.transpose(0, 1, 3, 2, 4).reshape(2, ex_dev, 4096)

    flat = load[:, :8].reshape(8, 2, 4, 2048).transpose(1, 0, 2, 3).reshape(2, 32, 2048)
    partial = jnp.einsum("mak,mbk->mab", flat, flat, preferred_element_type=F32)
    slot_ids = load[:, 8, :4, 0].reshape(32).astype(jnp.int32)
    labels = jnp.arange(32, dtype=jnp.int32)
    placing = (slot_ids[None, :] == labels[:, None]).astype(F32)
    by_id = jnp.einsum("as,mst,bt->mab", placing, partial, placing, precision=HIGHEST)
    gram = (by_id + swap_core(by_id)) / 4096.0
    norm = jnp.sqrt(jnp.sum(gram * jnp.eye(32, dtype=F32), axis=2) + 1e-06)
    picking = (queries[:, None] == labels[None, :]).astype(F32)
    chosen = jnp.einsum("qa,mab->mqb", picking, gram, precision=HIGHEST)
    chosen_norm = jnp.einsum("qa,ma->mq", picking, norm, precision=HIGHEST)
    scores = chosen / (chosen_norm[:, :, None] * norm[:, None, :])
    return projected, gram, scores


def solution(mesh):
    return jax.shard_map(
        body,
        mesh=mesh,
        in_specs=(
            P("dp", None, "tensor"),
            P("dp", None, "tensor"),
            P("dp", None, "tensor"),
            P("dp", None, None),
            P("tensor", "dp"),
            P("tensor", None),
            P(),
            P("tensor", None),
            P("tensor", None),
            P("dp"),
            P("dp"),
            P(),
        ),
        out_specs=(P(None, "dp", None), P(), P()),
        check_vma=False,
    )
```

```python
import functools

import jax
import jax.numpy as jnp
from jax import lax
from jax.experimental import pallas as pl
from jax.experimental.pallas import tpu as pltpu
from jax.sharding import PartitionSpec as P

AXES = ("dp", "tensor")
BF16, F32 = jnp.bfloat16, jnp.float32
HIGHEST = lax.Precision.HIGHEST
TILE = 512
EARLY_TILE = 256
NT = (((1,), (1,)), ((), ()))
CHUNKS = ((0, 896),)
VMEM_LIMIT = 60 * 2**20
BACK_LIMIT = 50 * 2**20
SHORT = pl.CostEstimate(flops=46 * 10**8, bytes_accessed=1000, transcendentals=0)
LONG = pl.CostEstimate(flops=10**11, bytes_accessed=10**8, transcendentals=0)


def coords(i):
    dp, tensor = divmod(i, 8)
    x_hi, rest = divmod(dp, 8)
    y, core = divmod(rest, 2)
    x_lo, z = divmod(tensor, 4)
    return x_hi * 2 + x_lo, y, z, core


def index(x, y, z, core):
    x_hi, x_lo = divmod(x % 4, 2)
    return ((x_hi * 4 + y % 4) * 2 + core) * 8 + x_lo * 4 + z % 4


def pair(v, phase):
    return (v ^ 1) if phase == 0 else (v + (1 if v % 2 else -1)) % 4


def moved(value, to):
    return lax.ppermute(value, AXES, [(i, index(*to(*coords(i)))) for i in range(128)])


def swap_core(v):
    return moved(v, lambda x, y, z, c: (x, y, z, 1 - c))


def swap_y(v, step):
    return moved(v, lambda x, y, z, c: (x, pair(y, step ^ c), z, c))


def swap_z(v, step):
    return moved(v, lambda x, y, z, c: (x, y, pair(z, step ^ c), c))


def swap_x(v, phase):
    return moved(v, lambda x, y, z, c: (pair(x, phase), y, z, c))


def swap_x_far(v):
    return moved(v, lambda x, y, z, c: (x + 2, y, z, c))


def silu(v):
    half = 0.5 * v
    return half + half * jnp.tanh(half)


def outer(left, right):
    left_hi, right_hi = left.astype(BF16), right.astype(BF16)
    left_lo = (left - left_hi.astype(F32)).astype(BF16)
    right_lo = (right - right_hi.astype(F32)).astype(BF16)
    sides = jnp.concatenate([left_hi, left_lo], axis=0), jnp.concatenate([right_hi, right_lo], axis=1)
    all_four = jnp.dot(*sides, preferred_element_type=F32)
    n, m = left.shape[0], right.shape[1]
    return all_four[:n, :m] + (all_four[:n, m:] + all_four[n:, :m]) + all_four[n:, m:]


def after(value, *others):
    def nothing(*refs):
        pass

    anywhere = pl.BlockSpec(memory_space=pl.ANY)
    return pl.pallas_call(
        nothing,
        out_shape=jax.ShapeDtypeStruct(value.shape, value.dtype),
        in_specs=[anywhere] * (1 + len(others)),
        out_specs=anywhere,
        input_output_aliases={0: 0},
        name="after",
    )(value, *others)


def added(left, right):
    def add(left, right, out):
        out[...] = left[...] + right[...]

    vmem = pl.BlockSpec(memory_space=pltpu.VMEM)
    return pl.pallas_call(
        add,
        out_shape=jax.ShapeDtypeStruct(left.shape, left.dtype),
        in_specs=[vmem, vmem],
        out_specs=vmem,
        cost_estimate=SHORT,
        name="added",
    )(left, right)


def rows_kernel(counts, gate, up, grad, inp, din_t, dout_t, uin_t, _, out):
    i = pl.program_id(0)
    per = 512 // EARLY_TILE
    act = silu(gate[...].astype(F32))
    hidden = (act * up[...].astype(F32)).astype(BF16)
    hid_t = lax.dot_general(din_t[...], hidden, NT, preferred_element_type=F32)
    in_t = lax.dot_general(uin_t[...], inp[...], NT, preferred_element_type=F32)
    out_rows = lax.dot_general(grad[...], dout_t[...], NT, preferred_element_type=F32)
    pos = (i % per) * EARLY_TILE + lax.broadcasted_iota(jnp.int32, (64, EARLY_TILE), 1)
    live = (pos < counts[i // per]).astype(F32)
    first = outer(hid_t * live, out_rows)
    packed = jnp.concatenate([first[:32], first[32:]], axis=1)
    here = pl.ds(pl.multiple_of((i // per) * 32, 32), 32)

    @pl.when(i % per == 0)
    def _():
        out[here, 1024:] = packed

    @pl.when(i % per != 0)
    def _():
        out[here, 1024:] += packed

    out[:, pl.ds(pl.multiple_of(i * EARLY_TILE, EARLY_TILE), EARLY_TILE)] = in_t * live


def projected_rows(counts, gate, up, grad, inp, din_t, dout_t, uin_t, later_than):
    tokens, width = gate.shape
    row = lambda n: pl.BlockSpec((EARLY_TILE, n), lambda i, s: (i, 0))
    full = lambda a: pl.BlockSpec(a.shape, lambda i, s: (0, 0))
    return pl.pallas_call(
        rows_kernel,
        out_shape=jax.ShapeDtypeStruct((64, tokens + 128), F32),
        grid_spec=pltpu.PrefetchScalarGridSpec(
            num_scalar_prefetch=1,
            grid=(tokens // EARLY_TILE,),
            in_specs=[row(width), row(width), row(grad.shape[1]), row(inp.shape[1]), full(din_t), full(dout_t), full(uin_t), pl.BlockSpec(memory_space=pl.ANY)],
            out_specs=pl.BlockSpec((64, tokens + 128), lambda i, s: (0, 0)),
        ),
        compiler_params=pltpu.CompilerParams(vmem_limit_bytes=VMEM_LIMIT),
        cost_estimate=LONG,
        name="early_rows",
    )(counts, gate, up, grad, inp, din_t, dout_t, uin_t, later_than)


def back_kernel(n, has_acc, last, lo, later, cols, *refs):
    i = pl.program_id(0)
    half = pl.num_programs(0) // 2
    refs = list(refs)
    if not last:
        refs.pop()[...] = jnp.zeros((8, 128), F32)
    acc_ref = refs.pop(0) if has_acc else None
    refs = refs[:len(refs) - 1 - later] + refs[-1:]
    blocks, rest = refs[: 3 * n], refs[3 * n :]
    out = rest[-1]

    def run(side):
        acc = acc_ref[...] if has_acc else None
        for p in range(n):
            term = lax.dot_general(blocks[3 * p + side][...], blocks[3 * p + 2][...], NT, preferred_element_type=F32)
            acc = term if acc is None else acc + term
        if not last:
            out[...] = acc
            return
        width = acc.shape[1]
        gate = rest[side][:, lo : lo + width]
        delta = (acc * silu(gate.astype(F32))).astype(BF16)
        del_rows = lax.dot_general(delta, rest[2][:, lo : lo + width], NT, preferred_element_type=F32)
        second = outer(rest[3 + 2 * side][...] + rest[4 + 2 * side][...], del_rows)
        packed = jnp.concatenate([second[:32], second[32:]], axis=1)

        @pl.when(i % (512 // TILE) == 0)
        def _():
            out[0] = packed

        @pl.when(i % (512 // TILE) != 0)
        def _():
            out[0] += packed

    @pl.when(i < half)
    def _():
        run(0)

    @pl.when(i >= half)
    def _():
        run(1)


def back_step(cols, acc, pieces, grads, tail=None, lo=0, later=(), cost=LONG):
    mine, theirs = grads
    tokens = mine.shape[0]
    steps = tokens // TILE
    width = pieces[0][0].shape[0]
    feats = pieces[0][0].shape[1]
    own_row = lambda i: jnp.minimum(i, steps - 1)
    other_row = lambda i: jnp.maximum(i - steps, 0)
    args, specs = [], []
    acc_spec = pl.BlockSpec((TILE, width), lambda i, s: (i, 0))
    if acc is not None:
        args.append(acc)
        specs.append(acc_spec)
    for weight, k in pieces:
        args += [mine, theirs, weight]
        specs += [
            pl.BlockSpec((TILE, feats), lambda i, s, k=k: (own_row(i), s[k])),
            pl.BlockSpec((TILE, feats), lambda i, s, k=k: (other_row(i), s[k])),
            pl.BlockSpec((width, feats), lambda i, s: (0, 0)),
        ]
    n = len(pieces)
    if tail is None:
        out_shape = (jax.ShapeDtypeStruct((2 * tokens, width), F32), jax.ShapeDtypeStruct((8, 128), F32))
        out_spec = (acc_spec, pl.BlockSpec((8, 128), lambda i, s: (0, 0)))
    else:
        hid = tail[0].shape[1] // 2
        args += tail
        mine_rows = pl.BlockSpec((64, TILE), lambda i, s: (0, own_row(i)))
        their_rows = pl.BlockSpec((64, TILE), lambda i, s: (0, other_row(i)))
        specs += [
            pl.BlockSpec((TILE, hid), lambda i, s: (own_row(i), s[8])),
            pl.BlockSpec((TILE, hid), lambda i, s: (other_row(i), s[8])),
            pl.BlockSpec((64, hid), lambda i, s: (0, s[8])),
            mine_rows,
            mine_rows,
            their_rows,
            their_rows,
        ]
        out_spec = pl.BlockSpec((1, 32, 128), lambda i, s: ((i // (512 // TILE) + 2 * s[8]) % 4, 0, 0))
        out_shape = jax.ShapeDtypeStruct((4, 32, 128), F32)
    args += later
    specs += [pl.BlockSpec(memory_space=pl.ANY)] * len(later)
    return pl.pallas_call(
        functools.partial(back_kernel, n, acc is not None, tail is not None, lo, len(later)),
        out_shape=out_shape,
        grid_spec=pltpu.PrefetchScalarGridSpec(
            num_scalar_prefetch=1, grid=(2 * steps,), in_specs=specs, out_specs=out_spec
        ),
        input_output_aliases={1: 0} if acc is not None and tail is None else {},
        compiler_params=pltpu.CompilerParams(vmem_limit_bytes=BACK_LIMIT),
        cost_estimate=cost,
        name="back_last" if tail is not None else "back_part",
    )(cols, *args)


def body(
    gate_pre, up_val, layer_in, out_grad, down_weight, down_in_proj, down_out_proj,
    up_in_proj, up_out_proj, counts, assignment, queries,
):
    ex_dev, seq_len, width_ff = gate_pre.shape
    tokens = ex_dev * seq_len
    half = width_ff // 2
    dp = lax.axis_index("dp")
    core = dp % 2
    y = (dp // 2) % 4
    x_hi = dp // 8

    def partner(v, step):
        odd = (step ^ core) == 0
        return jnp.where(odd, v ^ 1, (v + jnp.where(v % 2 == 1, 1, 3)) % 4)

    y1, y2 = partner(y, 0), partner(y, 1)
    y12 = partner(y2, 0)
    here, there = x_hi * 4, (1 - x_hi) * 4
    cols = jnp.stack(
        [here + y, here + y1, here + y2, there + y, here + y12, there + y2, there + y1, there + y12, core]
    ).astype(jnp.int32)

    gate = gate_pre.reshape(tokens, width_ff)
    up = up_val.reshape(tokens, width_ff)
    grads = out_grad.reshape(tokens, -1)
    inputs = layer_in.reshape(tokens, -1)

    weight_other = swap_core(down_weight)
    ids_other = swap_core(assignment)
    is_even = core == 0
    even = jnp.concatenate([down_weight[:half], weight_other[:half]], axis=1)
    odd = jnp.concatenate([weight_other[half:], down_weight[half:]], axis=1)
    h = jnp.where(is_even, even, odd)

    h_x = swap_x_far(h)
    h_y = swap_y(h, 0)
    h_y2 = swap_y(h, 1)
    early = projected_rows(
        counts, gate, up, grads, inputs, down_in_proj.T, down_out_proj.T, up_in_proj.T, h
    )
    grads_other = swap_core(grads)
    gate_other = swap_core(gate)
    both = (grads, grads_other)
    h_y = after(h_y, early)
    h_xy = swap_x_far(h_y)
    h_yy = swap_y(h_y, 1)
    rows = added(early, swap_z(early, 0))
    h_x, h_y2 = after(h_x, rows), after(h_y2, rows)
    h_xy2 = swap_y(h_x, 1)
    rows_second = swap_z(rows, 1)
    acc, done = back_step(cols, None, [(h, 0), (h_y, 1), (h_y2, 2), (h_x, 3)], both, later=(rows,), cost=SHORT)

    h_xy = after(h_xy, done)
    h_xyy = swap_y(h_xy, 1)
    rows = rows + after(rows_second, done)
    rows_x = swap_x(rows, 0)
    rows_core = swap_core(rows)
    rows_x_core = moved(rows, lambda x, y, z, c: (pair(x, 0), y, z, 1 - c))
    acc, _ = back_step(cols, acc, [(h_yy, 4), (h_xy2, 5), (h_xy, 6)], both, later=(rows,))
    tail = (gate, gate_other, up_out_proj.T, rows, rows_x, rows_core, rows_x_core)
    second = back_step(cols, acc, [(h_xyy, 7)], both, tail, 0)

    second_other = swap_core(second)
    mine = lax.dynamic_slice_in_dim(second + second_other, core * 16, 16, 1)
    mine = mine + swap_z(mine, 0)
    mine = mine + swap_z(mine, 1)
    mine = mine + swap_x(mine, 0)

    first = (rows[:, tokens:] + rows_x[:, tokens:]).reshape(ex_dev, 32, 128)
    first_other = (rows_core[:, tokens:] + rows_x_core[:, tokens:]).reshape(ex_dev, 32, 128)
    first_all = jnp.where(is_even, jnp.concatenate([first, first_other]), jnp.concatenate([first_other, first]))
    first_half = lax.dynamic_slice_in_dim(first_all, core * 16, 16, 1)
    ids = jnp.where(is_even, jnp.concatenate([assignment, ids_other]), jnp.concatenate([ids_other, assignment]))
    ids_block = jnp.broadcast_to(jnp.pad(ids, (0, 12))[None, :, None], (1, 16, 128)).astype(BF16)
    load = jnp.concatenate([first_half.astype(BF16), mine.astype(BF16), ids_block])
    load = jnp.stack([load, swap_x(load, 1)])
    load = jnp.concatenate([load, swap_y(load, 0)])
    load = jnp.concatenate([load, swap_y(load, 1)])

    mine_other = swap_core(mine)
    own = lax.dynamic_slice_in_dim(mine, core * ex_dev, ex_dev, 0)
    own_other = lax.dynamic_slice_in_dim(mine_other, core * ex_dev, ex_dev, 0)
    own_rows = jnp.where(is_even, jnp.concatenate([own, own_other], 1), jnp.concatenate([own_other, own], 1))
    out = jnp.stack([first, own_rows]).reshape(2, ex_dev, 32, 2, 64)
    projected = out.transpose(0, 1, 3, 2, 4).reshape(2, ex_dev, 4096)

    flat = load[:, :8].reshape(8, 2, 4, 2048).transpose(1, 0, 2, 3).reshape(2, 32, 2048)
    partial = jnp.einsum("mak,mbk->mab", flat, flat, preferred_element_type=F32)
    slot_ids = load[:, 8, :4, 0].reshape(32).astype(jnp.int32)
    labels = jnp.arange(32, dtype=jnp.int32)
    placing = (slot_ids[None, :] == labels[:, None]).astype(F32)
    by_id = jnp.einsum("as,mst,bt->mab", placing, partial, placing, precision=HIGHEST)
    gram = (by_id + swap_core(by_id)) / 4096.0
    norm = jnp.sqrt(jnp.sum(gram * jnp.eye(32, dtype=F32), axis=2) + 1e-06)
    picking = (queries[:, None] == labels[None, :]).astype(F32)
    chosen = jnp.einsum("qa,mab->mqb", picking, gram, precision=HIGHEST)
    chosen_norm = jnp.einsum("qa,ma->mq", picking, norm, precision=HIGHEST)
    scores = chosen / (chosen_norm[:, :, None] * norm[:, None, :])
    return projected, gram, scores


def solution(mesh):
    return jax.shard_map(
        body,
        mesh=mesh,
        in_specs=(
            P("dp", None, "tensor"),
            P("dp", None, "tensor"),
            P("dp", None, "tensor"),
            P("dp", None, None),
            P("tensor", "dp"),
            P("tensor", None),
            P(),
            P("tensor", None),
            P("tensor", None),
            P("dp"),
            P("dp"),
            P(),
        ),
        out_specs=(P(None, "dp", None), P(), P()),
        check_vma=False,
    )
```
